512 devices in a mesh: dom: 128 (over y, z, core), slab: 4 (over x).
Axes of the slice: x: 4, y: 4, z: 16, core: 2. Of those that a mesh axis runs over, the one named last changes fastest.
Arguments:
- node_feats: bfloat16 [131072, 512], P(('dom', 'slab')), may hold values from -6 to 6
- weight: bfloat16 [512, 512], replicated, may hold values from -0.25 to 0.25
- cotangent: bfloat16 [131072, 512], P(('dom', 'slab')), may hold values from -96 to 96
- degrees: int32 [131072], P(('dom', 'slab')), may hold values from 8 to 48
- local_weights: int32 [131072, 2, 128], P(('dom', 'slab')), may hold values from 0 to 3, as said below
- local_tiles: int32 [1024, 2], P(('dom', 'slab')), may hold values from 0 to 1
- send_rows: int32 [65536, 8], P(('dom', 'slab')), may hold values from 0 to 255
- send_count: int32 [65536], P(('dom', 'slab')), may hold values from 1 to 8, as said below
- recv_target: int32 [524288, 2], P(('dom', 'slab')), may hold values from 0 to 255
- recv_weight: int32 [524288, 2], P(('dom', 'slab')), may hold values from 1 to 3
Outputs:
- output: bfloat16 [131072, 512], P(('dom', 'slab'))
- grad_feats: bfloat16 [131072, 512], P(('dom', 'slab'))
- grad_weight: float32 [512, 512], replicated
The draws below stay inside these ranges and needn't reach their ends.
Inputs may be any that keep to these rules, and one draw needn't show every extreme that they name: Entry 0 of send_count is 8 and every entry is between 1 and 8; the live slots of a peer are the leading ones. `local_weights`: most entries are zero.
All inputs are finite; a program needn't handle non-finite values.
Results may differ from the reference program's by a relative error of at most 0.0062.
Values may be sent and summed in bfloat16 or wider, within the bound.
No kernel may reach another device: no remote copies, remote signals or barrier semaphores. Data moves between devices by JAX's collectives and lax.ppermute only.
A program may use at most 64 MiB of HBM per device.

```python
import math
import jax
import jax.numpy as jnp
from jax import lax

D = 512
ROWS = 256
TILE = 128
NB = 2
CAP = 8
KT = 2
NODES = 131072
N_DOM = 128
N_SLAB = 4


def draw_local_weights(key, part):
    key = jax.random.fold_in(key, 11)
    first, second = jax.random.split(key)
    present = jax.random.randint(first, (NODES, NB, TILE), 0, 16) == 0
    values = jax.random.randint(second, (NODES, NB, TILE), 1, 4)
    return jnp.where(present, values, 0).astype(jnp.int32)


def draw_send_count(key, part):
    key = jax.random.fold_in(key, 7)
    first, second = jax.random.split(key)
    total = NODES // ROWS * N_DOM
    spread = jax.random.randint(first, (total,), 1, CAP + 1)
    heavy = jax.random.randint(second, (total,), 0, 4) == 0
    counts = jnp.where(heavy, CAP, spread)
    counts = counts.at[0].set(CAP)
    return counts.astype(jnp.int32)


def touch_ends(values, rng, smallest, largest):
    shape = values.shape
    index_at = [jax.random.randint(jax.random.fold_in(rng, axis), (), 0, shape[axis]) for axis in range(len(shape))]
    values = values.at[tuple(index_at)].set(smallest)
    longest = shape.index(max(shape))
    index_at[longest] = (index_at[longest] + 1) % shape[longest]
    return values.at[tuple(index_at)].set(largest)


def raised(drawn, own_key, source, target, blocks, factor):
    owner, partner = [(jnp.arange(drawn.shape[position]) // (drawn.shape[position] // blocks)).reshape([-1 if axis == position else 1 for axis in range(drawn.ndim)]) for position in (source, target)]
    chosen = jax.random.permutation(own_key, blocks)[partner]
    strong = (owner == chosen) | (owner == (partner + blocks // 2) % blocks)
    return jnp.where(strong, factor * drawn, drawn)


def levels(own_key, shape, pieces, least, top_value):
    def one(axis_at, parts):
        steps = jax.random.uniform(jax.random.fold_in(jax.random.fold_in(own_key, 6), axis_at), (parts,), jnp.float32, least / len(pieces), top_value / len(pieces))
        return jnp.repeat(jnp.exp(steps), shape[axis_at] // parts).reshape((-1,) + (1,) * (len(shape) - axis_at - 1))

    loudness = one(*pieces[0])
    for cut in pieces[1:]:
        loudness = loudness * one(*cut)
    return loudness


def centred(rng, dims, deviation, bound, cuts=(), held_as=jnp.bfloat16):
    values = deviation * jax.random.normal(rng, dims, jnp.float32)
    if cuts:
        values = values * levels(rng, dims, cuts, -0.22, 0.18)
    return jnp.clip(values, -bound, bound).astype(held_as)


def noise_with(rng, shape, scale, limit, cuts, heavy, kind=jnp.bfloat16):
    result = scale * jax.random.normal(rng, shape, jnp.float32)
    if cuts:
        result = result * levels(rng, shape, cuts, -0.22, 0.18)
    return jnp.clip(raised(result, jax.random.fold_in(rng, 3), *heavy), -limit, limit).astype(kind)


def setup_inputs(seed: int = 0) -> dict:
    arg_keys = jax.random.split(jax.random.key(seed), 11)
    return {
        "node_feats": centred(arg_keys[0], (NODES, D), 1.0, 6.0, ((0, 512),)),
        "weight": centred(arg_keys[1], (D, D), D ** -0.5, 0.25),
        "cotangent": noise_with(arg_keys[2], (NODES, D), 4.0, 96.0, ((0, 512),), (0, 1, 512, 6.0)),
        "degrees": touch_ends(jax.random.randint(arg_keys[3], (NODES,), 8, 49), jax.random.fold_in(arg_keys[3], 1), 8, 48).astype(jnp.int32),
        "local_weights": draw_local_weights(jax.random.fold_in(arg_keys[10], 71), 0),
        "local_tiles": touch_ends(jax.random.randint(arg_keys[5], (NODES // TILE, NB), 0, ROWS // TILE), jax.random.fold_in(arg_keys[5], 1), 0, (ROWS // TILE) - 1).astype(jnp.int32),
        "send_rows": touch_ends(jax.random.randint(arg_keys[6], (NODES // ROWS * N_DOM, CAP), 0, ROWS), jax.random.fold_in(arg_keys[6], 1), 0, ROWS - 1).astype(jnp.int32),
        "send_count": draw_send_count(jax.random.fold_in(arg_keys[10], 71), 0),
        "recv_target": touch_ends(jax.random.randint(arg_keys[8], (NODES // ROWS * N_DOM * CAP, KT), 0, ROWS), jax.random.fold_in(arg_keys[8], 1), 0, ROWS - 1).astype(jnp.int32),
        "recv_weight": touch_ends(jax.random.randint(arg_keys[9], (NODES // ROWS * N_DOM * CAP, KT), 1, 4), jax.random.fold_in(arg_keys[9], 1), 1, 3).astype(jnp.int32),
    }


def reference(node_feats, weight, cotangent, degrees, local_weights, local_tiles, send_rows, send_count, recv_target, recv_weight):
    groups = N_DOM * N_SLAB
    tile_count = ROWS // TILE
    feats_dev = node_feats.reshape(groups, tile_count, TILE, D)
    tiles_dev = local_tiles.reshape(groups, tile_count, NB).astype(jnp.int32)
    weights_dev = local_weights.reshape(groups, tile_count, TILE, NB, TILE).astype(jnp.float32)

    def partition_forward(packed):
        tiles, edge_weight, feats = packed
        selected_rows = feats[tiles].astype(jnp.float32)
        reduced_sum = jnp.einsum('uqyr,uyrn->uqn', edge_weight, selected_rows, precision=lax.Precision.HIGHEST)
        return reduced_sum.reshape(ROWS, D)
    local_sum = lax.map(partition_forward, (tiles_dev, weights_dev, feats_dev)).reshape(NODES, D)
    local_sum = local_sum + node_feats.astype(jnp.float32)
    rows_view = send_rows.reshape(N_DOM, N_SLAB, N_DOM, CAP).astype(jnp.int32)
    count_view = send_count.reshape(N_DOM, N_SLAB, N_DOM)
    live_view = jnp.arange(CAP, dtype=jnp.int32)[None, None, None, :] < count_view[..., None]
    target_view = recv_target.reshape(N_DOM, N_SLAB, N_DOM, CAP, KT).astype(jnp.int32)
    edge_view = recv_weight.reshape(N_DOM, N_SLAB, N_DOM, CAP, KT).astype(jnp.float32)
    feats_view = node_feats.reshape(N_DOM, N_SLAB, ROWS, D)
    src_ids = jnp.arange(N_DOM, dtype=jnp.int32)[:, None, None]
    slab_ids = jnp.arange(N_SLAB, dtype=jnp.int32)[None, :, None]

    def remote_forward(dest):
        index = rows_view[:, :, dest]
        live = live_view[:, :, dest]
        sent = feats_view[src_ids, slab_ids, index].astype(jnp.float32)
        sent = jnp.where(live[..., None], sent, 0.0)
        sent = jnp.transpose(sent, (1, 0, 2, 3))
        edge_contribution = sent[:, :, :, None, :] * edge_view[dest][..., None]
        segment_index = (slab_ids.reshape(N_SLAB, 1, 1, 1) * ROWS + target_view[dest]).astype(jnp.int32)
        reduced_sum = jax.ops.segment_sum(edge_contribution.reshape(-1, D), segment_index.reshape(-1), num_segments=N_SLAB * ROWS)
        return reduced_sum.reshape(N_SLAB, ROWS, D)
    remote = lax.map(remote_forward, jnp.arange(N_DOM, dtype=jnp.int32)).reshape(NODES, D)
    inv_degree = 1.0 / degrees.astype(jnp.float32)
    aggregated = ((local_sum + remote) * inv_degree[:, None]).astype(jnp.bfloat16)
    pre_act = jnp.dot(aggregated, weight, preferred_element_type=jnp.float32)
    gating_value = jax.nn.sigmoid(pre_act)
    output = (pre_act * gating_value).astype(jnp.bfloat16)
    grad_pre = (cotangent.astype(jnp.float32) * gating_value * (1.0 + pre_act * (1.0 - gating_value))).astype(jnp.bfloat16)
    grad_weight = jnp.dot(aggregated.T, grad_pre, preferred_element_type=jnp.float32) * (1.0 / math.sqrt(NODES))
    grad_sum = (jnp.dot(grad_pre, weight.T, preferred_element_type=jnp.float32) * inv_degree[:, None]).astype(jnp.bfloat16)
    grad_dev = grad_sum.reshape(groups, tile_count, TILE, D)

    def local_backward(packed):
        tiles, edge_weight, gradient_list = packed
        edge_contribution = jnp.einsum('gxsn,gxh->gsnh', edge_weight, gradient_list.astype(jnp.float32), precision=lax.Precision.HIGHEST)
        reduced_sum = jax.ops.segment_sum(edge_contribution.reshape(tile_count * NB, TILE, D), tiles.reshape(-1), num_segments=tile_count)
        return reduced_sum.reshape(ROWS, D)
    local_back = lax.map(local_backward, (tiles_dev, weights_dev, grad_dev)).reshape(NODES, D)
    local_back = local_back + grad_sum.astype(jnp.float32)
    dest_ids = jnp.arange(N_DOM, dtype=jnp.int32)[:, None, None, None]
    slab_grid = jnp.arange(N_SLAB, dtype=jnp.int32)[None, :, None, None]

    def remote_backward(source):
        targets = target_view[:, :, source]
        edges = edge_view[:, :, source]
        global_ids = ((dest_ids * N_SLAB + slab_grid) * ROWS + targets).astype(jnp.int32)
        selected_rows = grad_sum[global_ids].astype(jnp.float32)
        slot_grad = lax.optimization_barrier(jnp.sum(selected_rows * edges[..., None], axis=3)).astype(jnp.bfloat16).astype(jnp.float32)
        slot_grad = jnp.transpose(slot_grad, (1, 0, 2, 3))
        live = live_view[source]
        slot_grad = jnp.where(live[..., None], slot_grad, 0.0)
        owner_ids = (jnp.arange(N_SLAB, dtype=jnp.int32)[:, None, None] * ROWS + rows_view[source]).astype(jnp.int32)
        reduced_sum = jax.ops.segment_sum(slot_grad.reshape(-1, D), owner_ids.reshape(-1), num_segments=N_SLAB * ROWS)
        return reduced_sum.reshape(N_SLAB, ROWS, D)
    remote_back = lax.map(remote_backward, jnp.arange(N_DOM, dtype=jnp.int32)).reshape(NODES, D)
    grad_feats = (local_back + remote_back).astype(jnp.bfloat16)
    return (output, grad_feats, grad_weight)
```

```python
import math

import jax
import jax.numpy as jnp
from jax import lax
from jax.sharding import Mesh
from jax.sharding import PartitionSpec as P


DOM = ("y", "z", "core")
PLANE = ("y", "core", "slab")


def reduce_everywhere(part, scale):
    rows, width = part.shape
    plane, depth = lax.axis_size(PLANE), lax.axis_size("z")
    pieces = part.astype(jnp.bfloat16).reshape(plane, rows // plane, width)
    pieces = lax.all_to_all(pieces, PLANE, split_axis=0, concat_axis=0, tiled=True)
    mine = jnp.sum(pieces.astype(jnp.float32), axis=0)
    mine = mine.reshape(depth, rows // plane // depth, width)
    mine = lax.all_to_all(mine, "z", split_axis=0, concat_axis=0, tiled=True)
    mine = jnp.sum(mine, axis=0, keepdims=True) * scale
    mine = jnp.broadcast_to(mine, (depth,) + mine.shape[1:])
    mine = lax.all_to_all(mine, "z", split_axis=0, concat_axis=0, tiled=True)
    mine = mine.reshape(1, rows // plane, width).astype(jnp.bfloat16)
    mine = jnp.broadcast_to(mine, (plane,) + mine.shape[1:])
    whole = lax.all_to_all(mine, PLANE, split_axis=0, concat_axis=0, tiled=True)
    return whole.reshape(rows, width).astype(jnp.float32)


def shards(
    node_feats,
    weight,
    cotangent,
    degrees,
    local_weights,
    local_tiles,
    send_rows,
    send_count,
    recv_target,
    recv_weight,
):
    row_count, feat_width = node_feats.shape
    tile_size = local_weights.shape[2]
    tile_count = row_count // tile_size
    listed = local_tiles.shape[1]
    peer_count = lax.axis_size(DOM)
    slot_cap = send_rows.shape[1]
    slot_count = peer_count * slot_cap
    nodes_all = row_count * lax.axis_size(DOM + ("slab",))
    column_ids = jnp.arange(tile_count, dtype=jnp.int32)
    selector = (local_tiles[:, :, None] == column_ids[None, None, :]).astype(jnp.bfloat16)
    blocks = local_weights.reshape(tile_count, tile_size, listed, tile_size).astype(jnp.bfloat16)
    adjacency = jnp.einsum("ikj,iakb->iajb", selector, blocks, preferred_element_type=jnp.float32)
    adjacency = adjacency.reshape(row_count, row_count).astype(jnp.bfloat16)
    live_slot = jnp.arange(slot_cap, dtype=jnp.int32)[None, :] < send_count[:, None]
    flat_rows = send_rows.reshape(-1)
    outgoing = jnp.take(node_feats, flat_rows, axis=0).reshape(peer_count, slot_cap, feat_width)
    outgoing = jnp.where(live_slot[:, :, None], outgoing, jnp.zeros((), jnp.bfloat16))
    incoming = lax.all_to_all(outgoing, DOM, split_axis=0, concat_axis=0, tiled=True).reshape(
        slot_count, feat_width
    )
    local_sum = jnp.dot(
        adjacency, node_feats, preferred_element_type=jnp.float32
    ) + node_feats.astype(jnp.float32)
    row_ids = jnp.arange(row_count, dtype=jnp.int32)
    mixing = jnp.sum(
        jnp.where(row_ids[:, None, None] == recv_target[None, :, :], recv_weight[None, :, :], 0),
        axis=2,
    )
    mixing = mixing.astype(jnp.bfloat16)
    remote = jnp.dot(mixing, incoming, preferred_element_type=jnp.float32)
    inv_degree = 1.0 / degrees.astype(jnp.float32)
    aggregated = ((local_sum + remote) * inv_degree[:, None]).astype(jnp.bfloat16)
    pre_act = jnp.dot(aggregated, weight, preferred_element_type=jnp.float32)
    gating_value = jax.nn.sigmoid(pre_act)
    output = (pre_act * gating_value).astype(jnp.bfloat16)
    grad_pre = (
        cotangent.astype(jnp.float32) * gating_value * (1.0 + pre_act * (1.0 - gating_value))
    ).astype(jnp.bfloat16)
    weight_part = lax.dot_general(
        aggregated, grad_pre, (((0,), (0,)), ((), ())), preferred_element_type=jnp.float32
    )
    grad_weight = reduce_everywhere(weight_part, 1.0 / math.sqrt(nodes_all))
    grad_sum = lax.dot_general(
        grad_pre, weight, (((1,), (1,)), ((), ())), preferred_element_type=jnp.float32
    )
    grad_sum = (grad_sum * inv_degree[:, None]).astype(jnp.bfloat16)
    slot_grad = lax.dot_general(
        mixing, grad_sum, (((0,), (0,)), ((), ())), preferred_element_type=jnp.float32
    )
    slot_grad = slot_grad.astype(jnp.bfloat16).reshape(peer_count, slot_cap, feat_width)
    returned = lax.all_to_all(slot_grad, DOM, split_axis=0, concat_axis=0, tiled=True)
    returned = jnp.where(live_slot[:, :, None], returned, jnp.zeros((), jnp.bfloat16)).reshape(
        slot_count, feat_width
    )
    local_back = lax.dot_general(
        adjacency, grad_sum, (((0,), (0,)), ((), ())), preferred_element_type=jnp.float32
    )
    local_back = local_back + grad_sum.astype(jnp.float32)
    owner_map = (row_ids[:, None] == flat_rows[None, :]).astype(jnp.bfloat16)
    remote_back = jnp.dot(owner_map, returned, preferred_element_type=jnp.float32)
    grad_feats = (local_back + remote_back).astype(jnp.bfloat16)
    return (output, grad_feats, grad_weight)


def solution(mesh):
    slab_count = mesh.shape["slab"]
    depth = mesh.shape["dom"] // (2 * slab_count)
    split = Mesh(
        mesh.devices.reshape(slab_count, depth, 2, slab_count), ("y", "z", "core", "slab")
    )
    nodes = P(DOM + ("slab",))
    in_specs = (nodes, P(), nodes, nodes, nodes, nodes, nodes, nodes, nodes, nodes)
    out_specs = (nodes, nodes, P())
    return jax.shard_map(shards, mesh=split, in_specs=in_specs, out_specs=out_specs, check_vma=False)
```

```python
import math

import jax
import jax.numpy as jnp
from jax import lax
from jax.sharding import Mesh
from jax.sharding import PartitionSpec as P


DOM = ("y", "z", "core")


def from_peer(value, axis, mask):
    count = lax.axis_size(axis)
    return lax.ppermute(value, axis, [(place, place ^ mask) for place in range(count)])


def scatter_sum(part, axis):
    count, here = lax.axis_size(axis), lax.axis_index(axis)
    rows = part.shape[0] // count
    total = lax.dynamic_slice_in_dim(part, here * rows, rows)
    for mask in range(1, count):
        block = lax.dynamic_slice_in_dim(part, (here ^ mask) * rows, rows)
        total = total + from_peer(block.astype(jnp.bfloat16), axis, mask).astype(jnp.float32)
    return total


def quad_sum(value, axis, stride):
    near = value + from_peer(value, axis, stride)
    far = from_peer(value, axis, 2 * stride) + from_peer(value, axis, 3 * stride)
    return near + far


def gather(block, axis):
    count, here = lax.axis_size(axis), lax.axis_index(axis)
    rows, width = block.shape
    whole = jnp.zeros((count * rows, width), block.dtype)
    whole = lax.dynamic_update_slice_in_dim(whole, block, here * rows, 0)
    for mask in range(1, count):
        other = from_peer(block, axis, mask)
        whole = lax.dynamic_update_slice_in_dim(whole, other, (here ^ mask) * rows, 0)
    return whole


PLANE = ("core", "slab", "y")


def sum_blocks(part, scale):
    mine = scatter_sum(scatter_sum(scatter_sum(part, "core"), "slab"), "y")
    return (quad_sum(quad_sum(mine, "z", 4), "z", 1) * scale).astype(jnp.bfloat16)


def gather_plane(mine):
    plane = lax.axis_size(PLANE)
    mine = jnp.broadcast_to(mine[None], (plane,) + mine.shape)
    whole = lax.all_to_all(mine, PLANE, split_axis=0, concat_axis=0, tiled=True)
    return whole.reshape(-1, mine.shape[-1]).astype(jnp.float32)


def shards(
    node_feats,
    weight,
    cotangent,
    degrees,
    local_weights,
    local_tiles,
    send_rows,
    send_count,
    recv_target,
    recv_weight,
):
    row_count, feat_width = node_feats.shape
    tile_size = local_weights.shape[2]
    tile_count = row_count // tile_size
    listed = local_tiles.shape[1]
    peer_count = lax.axis_size(DOM)
    slot_cap = send_rows.shape[1]
    slot_count = peer_count * slot_cap
    nodes_all = row_count * lax.axis_size(DOM + ("slab",))
    column_ids = jnp.arange(tile_count, dtype=jnp.int32)
    selector = (local_tiles[:, :, None] == column_ids[None, None, :]).astype(jnp.bfloat16)
    blocks = local_weights.reshape(tile_count, tile_size, listed, tile_size).astype(jnp.bfloat16)
    adjacency = jnp.einsum("ikj,iakb->iajb", selector, blocks, preferred_element_type=jnp.float32)
    adjacency = adjacency.reshape(row_count, row_count).astype(jnp.bfloat16)
    live_slot = jnp.arange(slot_cap, dtype=jnp.int32)[None, :] < send_count[:, None]
    row_ids = jnp.arange(row_count, dtype=jnp.int32)
    slot_ids = jnp.arange(slot_count, dtype=jnp.int32)
    live_rows = jnp.where(live_slot, send_rows, row_count).astype(jnp.bfloat16)
    to_slot = jnp.arange(peer_count, dtype=jnp.int32)[:, None] == slot_ids[None, :] // slot_cap
    spread = lax.dot_general(
        live_rows,
        to_slot.astype(jnp.bfloat16),
        (((0,), (0,)), ((), ())),
        preferred_element_type=jnp.float32,
    )
    own_column = jnp.arange(slot_cap, dtype=jnp.int32)[:, None] == slot_ids[None, :] % slot_cap
    flat_rows = jnp.sum(jnp.where(own_column, spread, 0.0), axis=0)
    owner = (row_ids[:, None] == flat_rows.astype(jnp.int32)[None, :]).astype(jnp.bfloat16)
    outgoing = lax.dot_general(
        owner, node_feats, (((0,), (0,)), ((), ())), preferred_element_type=jnp.float32
    )
    outgoing = outgoing.astype(jnp.bfloat16).reshape(peer_count, slot_cap, feat_width)
    incoming = lax.all_to_all(outgoing, DOM, split_axis=0, concat_axis=0, tiled=True).reshape(
        slot_count, feat_width
    )
    local_sum = jnp.dot(
        adjacency, node_feats, preferred_element_type=jnp.float32
    ) + node_feats.astype(jnp.float32)
    mixing = jnp.sum(
        jnp.where(row_ids[:, None, None] == recv_target[None, :, :], recv_weight[None, :, :], 0),
        axis=2,
    )
    mixing = mixing.astype(jnp.bfloat16)
    remote = jnp.dot(mixing, incoming, preferred_element_type=jnp.float32)
    inv_degree = 1.0 / degrees.astype(jnp.float32)
    aggregated = ((local_sum + remote) * inv_degree[:, None]).astype(jnp.bfloat16)
    pre_act = jnp.dot(aggregated, weight, preferred_element_type=jnp.float32)
    gating_value = jax.nn.sigmoid(pre_act)
    output = (pre_act * gating_value).astype(jnp.bfloat16)
    grad_pre = (
        cotangent.astype(jnp.float32) * gating_value * (1.0 + pre_act * (1.0 - gating_value))
    ).astype(jnp.bfloat16)
    grad_sum = lax.dot_general(
        grad_pre, weight, (((1,), (1,)), ((), ())), preferred_element_type=jnp.float32
    )
    grad_sum = (grad_sum * inv_degree[:, None]).astype(jnp.bfloat16)
    slot_grad = lax.dot_general(
        mixing, grad_sum, (((0,), (0,)), ((), ())), preferred_element_type=jnp.float32
    )
    slot_grad = slot_grad.astype(jnp.bfloat16).reshape(peer_count, slot_cap, feat_width)
    slot_grad, aggregated = lax.optimization_barrier((slot_grad, aggregated))
    returned = lax.all_to_all(slot_grad, DOM, split_axis=0, concat_axis=0, tiled=True)
    returned = returned.reshape(slot_count, feat_width)
    weight_part = lax.dot_general(
        aggregated, grad_pre, (((0,), (0,)), ((), ())), preferred_element_type=jnp.float32
    )
    mine = sum_blocks(weight_part, 1.0 / math.sqrt(nodes_all))
    returned, mine = lax.optimization_barrier((returned, mine))
    grad_weight = gather_plane(mine)
    local_back = lax.dot_general(
        adjacency, grad_sum, (((0,), (0,)), ((), ())), preferred_element_type=jnp.float32
    )
    local_back = local_back + grad_sum.astype(jnp.float32)
    remote_back = jnp.dot(owner, returned, preferred_element_type=jnp.float32)
    grad_feats = (local_back + remote_back).astype(jnp.bfloat16)
    return (output, grad_feats, grad_weight)


def solution(mesh):
    slab_count = mesh.shape["slab"]
    depth = mesh.shape["dom"] // (2 * slab_count)
    split = Mesh(
        mesh.devices.reshape(slab_count, depth, 2, slab_count), ("y", "z", "core", "slab")
    )
    nodes = P(DOM + ("slab",))
    in_specs = (nodes, P(), nodes, nodes, nodes, nodes, nodes, nodes, nodes, nodes)
    out_specs = (nodes, nodes, P())
    return jax.shard_map(shards, mesh=split, in_specs=in_specs, out_specs=out_specs, check_vma=False)
```

```python
import math

import jax
import jax.numpy as jnp
from jax import lax
from jax.sharding import Mesh
from jax.sharding import PartitionSpec as P


DOM = ("y", "z_hi", "z_lo", "core")


def from_peer(value, axis, mask):
    count = lax.axis_size(axis)
    return lax.ppermute(value, axis, [(place, place ^ mask) for place in range(count)])


def scatter_sum(part, axis):
    count, here = lax.axis_size(axis), lax.axis_index(axis)
    rows = part.shape[0] // count
    total = lax.dynamic_slice_in_dim(part, here * rows, rows)
    for mask in range(1, count):
        block = lax.dynamic_slice_in_dim(part, (here ^ mask) * rows, rows)
        total = total + from_peer(block.astype(jnp.bfloat16), axis, mask).astype(jnp.float32)
    return total


def quad_sum(value, axis):
    near = value + from_peer(value, axis, 1)
    return near + (from_peer(value, axis, 2) + from_peer(value, axis, 3))


def to_all(value, axes):
    count = lax.axis_size(axes)
    value = jnp.broadcast_to(value[None], (count,) + value.shape)
    return lax.all_to_all(value, axes, split_axis=0, concat_axis=0, tiled=True)


PLANE = ("core", "slab", "y")


def sum_blocks(part):
    mine = scatter_sum(scatter_sum(scatter_sum(part, "core"), "slab"), "y")
    return quad_sum(mine, "z_hi")


def finish_sum(mine, scale):
    mine = (jnp.sum(to_all(mine, "z_lo"), axis=0) * scale).astype(jnp.bfloat16)
    return to_all(mine, PLANE).reshape(-1, mine.shape[-1]).astype(jnp.float32)


def shards(
    node_feats,
    weight,
    cotangent,
    degrees,
    local_weights,
    local_tiles,
    send_rows,
    send_count,
    recv_target,
    recv_weight,
):
    row_count, feat_width = node_feats.shape
    tile_size = local_weights.shape[2]
    tile_count = row_count // tile_size
    listed = local_tiles.shape[1]
    peer_count = lax.axis_size(DOM)
    slot_cap = send_rows.shape[1]
    slot_count = peer_count * slot_cap
    nodes_all = row_count * lax.axis_size(DOM + ("slab",))
    column_ids = jnp.arange(tile_count, dtype=jnp.int32)
    selector = (local_tiles[:, :, None] == column_ids[None, None, :]).astype(jnp.bfloat16)
    blocks = local_weights.reshape(tile_count, tile_size, listed, tile_size).astype(jnp.bfloat16)
    adjacency = jnp.einsum("ikj,iakb->iajb", selector, blocks, preferred_element_type=jnp.float32)
    adjacency = adjacency.reshape(row_count, row_count).astype(jnp.bfloat16)
    live_slot = jnp.arange(slot_cap, dtype=jnp.int32)[None, :] < send_count[:, None]
    row_ids = jnp.arange(row_count, dtype=jnp.int32)
    slot_ids = jnp.arange(slot_count, dtype=jnp.int32)
    live_rows = jnp.where(live_slot, send_rows, row_count).astype(jnp.bfloat16)
    to_slot = jnp.arange(peer_count, dtype=jnp.int32)[:, None] == slot_ids[None, :] // slot_cap
    spread = lax.dot_general(
        live_rows,
        to_slot.astype(jnp.bfloat16),
        (((0,), (0,)), ((), ())),
        preferred_element_type=jnp.float32,
    )
    own_column = jnp.arange(slot_cap, dtype=jnp.int32)[:, None] == slot_ids[None, :] % slot_cap
    flat_rows = jnp.sum(jnp.where(own_column, spread, 0.0), axis=0)
    owner = (row_ids[:, None] == flat_rows.astype(jnp.int32)[None, :]).astype(jnp.bfloat16)
    outgoing = lax.dot_general(
        owner, node_feats, (((0,), (0,)), ((), ())), preferred_element_type=jnp.float32
    )
    outgoing = outgoing.astype(jnp.bfloat16).reshape(peer_count, slot_cap, feat_width)
    incoming = lax.all_to_all(outgoing, DOM, split_axis=0, concat_axis=0, tiled=True).reshape(
        slot_count, feat_width
    )
    local_sum = jnp.dot(
        adjacency, node_feats, preferred_element_type=jnp.float32
    ) + node_feats.astype(jnp.float32)
    mixing = jnp.sum(
        jnp.where(row_ids[:, None, None] == recv_target[None, :, :], recv_weight[None, :, :], 0),
        axis=2,
    )
    mixing = mixing.astype(jnp.bfloat16)
    remote = jnp.dot(mixing, incoming, preferred_element_type=jnp.float32)
    inv_degree = 1.0 / degrees.astype(jnp.float32)
    aggregated = ((local_sum + remote) * inv_degree[:, None]).astype(jnp.bfloat16)
    pre_act = jnp.dot(aggregated, weight, preferred_element_type=jnp.float32)
    gating_value = jax.nn.sigmoid(pre_act)
    output = (pre_act * gating_value).astype(jnp.bfloat16)
    grad_pre = (
        cotangent.astype(jnp.float32) * gating_value * (1.0 + pre_act * (1.0 - gating_value))
    ).astype(jnp.bfloat16)
    grad_sum = lax.dot_general(
        grad_pre, weight, (((1,), (1,)), ((), ())), preferred_element_type=jnp.float32
    )
    grad_sum = (grad_sum * inv_degree[:, None]).astype(jnp.bfloat16)
    slot_grad = lax.dot_general(
        mixing, grad_sum, (((0,), (0,)), ((), ())), preferred_element_type=jnp.float32
    )
    slot_grad = slot_grad.astype(jnp.bfloat16).reshape(peer_count, slot_cap, feat_width)
    slot_grad, aggregated = lax.optimization_barrier((slot_grad, aggregated))
    returned = lax.all_to_all(slot_grad, DOM, split_axis=0, concat_axis=0, tiled=True)
    returned = returned.reshape(slot_count, feat_width)
    weight_part = lax.dot_general(
        aggregated, grad_pre, (((0,), (0,)), ((), ())), preferred_element_type=jnp.float32
    )
    mine = sum_blocks(weight_part)
    returned, mine = lax.optimization_barrier((returned, mine))
    grad_weight = finish_sum(mine, 1.0 / math.sqrt(nodes_all))
    local_back = lax.dot_general(
        adjacency, grad_sum, (((0,), (0,)), ((), ())), preferred_element_type=jnp.float32
    )
    local_back = local_back + grad_sum.astype(jnp.float32)
    remote_back = jnp.dot(owner, returned, preferred_element_type=jnp.float32)
    grad_feats = (local_back + remote_back).astype(jnp.bfloat16)
    return (output, grad_feats, grad_weight)


def solution(mesh):
    slab_count = mesh.shape["slab"]
    split = Mesh(
        mesh.devices.reshape(4, 4, -1, 2, slab_count), ("y", "z_hi", "z_lo", "core", "slab")
    )
    nodes = P(DOM + ("slab",))
    in_specs = (nodes, P(), nodes, nodes, nodes, nodes, nodes, nodes, nodes, nodes)
    out_specs = (nodes, nodes, P())
    return jax.shard_map(shards, mesh=split, in_specs=in_specs, out_specs=out_specs, check_vma=False)
```

```python
import math

import jax
import jax.numpy as jnp
from jax import lax
from jax.experimental import pallas as pl
from jax.experimental.pallas import tpu as pltpu
from jax.sharding import Mesh
from jax.sharding import PartitionSpec as P


DOM = ("y", "z_hi", "z_lo", "core")


def from_peer(value, axis, mask):
    count = lax.axis_size(axis)
    return lax.ppermute(value, axis, [(place, place ^ mask) for place in range(count)])


def scatter_sum(part, axis):
    count, here = lax.axis_size(axis), lax.axis_index(axis)
    rows = part.shape[0] // count
    total = lax.dynamic_slice_in_dim(part, here * rows, rows)
    for mask in range(1, count):
        block = lax.dynamic_slice_in_dim(part, (here ^ mask) * rows, rows)
        total = total + from_peer(block.astype(jnp.bfloat16), axis, mask).astype(jnp.float32)
    return total


def quad_sum(value, axis):
    near = value + from_peer(value, axis, 1)
    return near + (from_peer(value, axis, 2) + from_peer(value, axis, 3))


def to_all(value, axes):
    count = lax.axis_size(axes)
    value = jnp.broadcast_to(value[None], (count,) + value.shape)
    return lax.all_to_all(value, axes, split_axis=0, concat_axis=0, tiled=True)


PLANE = ("core", "slab", "y")


def sum_blocks(part):
    mine = scatter_sum(scatter_sum(scatter_sum(part, "core"), "slab"), "y")
    return quad_sum(mine, "z_hi")


def finish_sum(mine, scale):
    mine = (jnp.sum(to_all(mine, "z_lo"), axis=0) * scale).astype(jnp.bfloat16)
    return to_all(mine, PLANE).reshape(-1, mine.shape[-1]).astype(jnp.float32)


VMEM = pl.BlockSpec(memory_space=pltpu.VMEM)
HBM = pl.BlockSpec(memory_space=pltpu.HBM)
PARTS = 4


def layer_kernel(
    incoming, mixing, mixing_rows, local_sum, inv_degree, weight, cotangent,
    output, aggregated, grad_pre, grad_sum, slot_grad,
    output_rows, aggregated_rows, grad_rows, summed_rows, slots, done,
):
    copies = []

    def leave(source, target):
        copy = pltpu.make_async_copy(source, target, done.at[len(copies)])
        copy.start()
        copies.append(copy)

    inverse = inv_degree[...]
    remote = jnp.dot(mixing[...], incoming[...], preferred_element_type=jnp.float32)
    gathered = ((local_sum[...] + remote) * inverse).astype(jnp.bfloat16)
    aggregated_rows[...] = gathered
    leave(aggregated_rows, aggregated)
    pre_act = jnp.dot(gathered, weight[...], preferred_element_type=jnp.float32)
    gating_value = jax.nn.sigmoid(pre_act)
    output_rows[...] = (pre_act * gating_value).astype(jnp.bfloat16)
    leave(output_rows, output)
    scaled = cotangent[...].astype(jnp.float32) * gating_value
    grad = (scaled * (1.0 + pre_act * (1.0 - gating_value))).astype(jnp.bfloat16)
    grad_rows[...] = grad
    leave(grad_rows, grad_pre)
    summed = lax.dot_general(
        grad, weight[...], (((1,), (1,)), ((), ())), preferred_element_type=jnp.float32
    )
    summed = (summed * inverse).astype(jnp.bfloat16)
    summed_rows[...] = summed
    leave(summed_rows, grad_sum)
    rows = slots.shape[0] // PARTS
    for part in range(PARTS):
        span = pl.ds(part * rows, rows)
        slots[span, :] = jnp.dot(
            mixing_rows[span, :], summed, preferred_element_type=jnp.float32
        ).astype(jnp.bfloat16)
        leave(slots.at[span, :], slot_grad.at[span, :])
    for copy in copies:
        copy.wait()


def layer(incoming, mixing, local_sum, inv_degree, weight, cotangent):
    nodes, slot_count = mixing.shape
    width = weight.shape[0]
    rows = pltpu.HBM((nodes, width), jnp.bfloat16)
    return pl.pallas_call(
        layer_kernel,
        out_shape=(rows, rows, rows, rows, pltpu.HBM((slot_count, width), jnp.bfloat16)),
        in_specs=[VMEM] * 7,
        out_specs=(HBM,) * 5,
        scratch_shapes=[pltpu.VMEM((nodes, width), jnp.bfloat16)] * 4
        + [
            pltpu.VMEM((slot_count, width), jnp.bfloat16),
            pltpu.SemaphoreType.DMA((4 + PARTS,)),
        ],
        compiler_params=pltpu.CompilerParams(vmem_limit_bytes=24 << 20),
        cost_estimate=pl.CostEstimate(
            flops=2 * nodes * width * (2 * slot_count + 2 * width),
            bytes_accessed=6 << 20,
            transcendentals=nodes * width,
        ),
        name="layer",
    )(incoming, mixing, mixing.T, local_sum, inv_degree[:, None], weight, cotangent)


def take_kernel(
    send_rows, send_count, node_feats, outgoing, row_table, counts, feats, taken, ready, done
):
    arrivals = []
    for at, (source, target) in enumerate(
        ((send_rows, row_table), (send_count, counts), (node_feats, feats))
    ):
        copy = pltpu.make_async_copy(source, target, ready.at[at])
        copy.start()
        arrivals.append(copy)
    slot_cap, peer_count = row_table.shape
    nodes, slot_count = feats.shape[0], taken.shape[0]
    slot = lax.broadcasted_iota(jnp.int32, (slot_count, peer_count), 0)
    first = slot_cap * lax.broadcasted_iota(jnp.int32, (slot_count, peer_count), 1)
    place = jnp.where((slot >= first) & (slot < first + slot_cap), 1.0, 0.0)
    slot = lax.broadcasted_iota(jnp.int32, (slot_count, slot_cap), 0)
    column = lax.rem(slot, slot_cap) == lax.broadcasted_iota(jnp.int32, slot.shape, 1)
    arrivals[0].wait()
    arrivals[1].wait()
    rank = lax.broadcasted_iota(jnp.int32, (slot_cap, peer_count), 0)
    live = jnp.where(rank < counts[...], row_table[...], nodes).astype(jnp.float32)
    spread = lax.dot_general(
        place.astype(jnp.bfloat16),
        live.astype(jnp.bfloat16),
        (((1,), (1,)), ((), ())),
        preferred_element_type=jnp.float32,
    )
    spread = jnp.where(column, spread, 0.0).astype(jnp.bfloat16)
    row = jnp.dot(
        spread, jnp.ones((slot_cap, nodes), jnp.bfloat16), preferred_element_type=jnp.float32
    )
    node = lax.broadcasted_iota(jnp.int32, row.shape, 1).astype(jnp.float32)
    chosen = jnp.where(row == node, 1.0, 0.0).astype(jnp.bfloat16)
    arrivals[2].wait()
    rows = slot_count // PARTS
    copies = []
    for part in range(PARTS):
        span = pl.ds(part * rows, rows)
        taken[span, :] = jnp.dot(
            chosen[part * rows : (part + 1) * rows], feats[...], preferred_element_type=jnp.float32
        ).astype(jnp.bfloat16)
        copy = pltpu.make_async_copy(taken.at[span, :], outgoing.at[span, :], done.at[part])
        copy.start()
        copies.append(copy)
    for copy in copies:
        copy.wait()


def take_rows(send_rows, send_count, node_feats):
    peer_count, slot_cap = send_rows.shape
    nodes, width = node_feats.shape
    slots = jax.ShapeDtypeStruct((peer_count * slot_cap, width), jnp.bfloat16)
    return pl.pallas_call(
        take_kernel,
        out_shape=slots,
        in_specs=[HBM] * 3,
        out_specs=HBM,
        scratch_shapes=[
            pltpu.VMEM((slot_cap, peer_count), jnp.int32),
            pltpu.VMEM((1, peer_count), jnp.int32),
            pltpu.VMEM((nodes, width), jnp.bfloat16),
            pltpu.VMEM(slots.shape, slots.dtype),
            pltpu.SemaphoreType.DMA((3,)),
            pltpu.SemaphoreType.DMA((PARTS,)),
        ],
        compiler_params=pltpu.CompilerParams(vmem_limit_bytes=63_400_000),
        cost_estimate=pl.CostEstimate(
            flops=2 * nodes * width * peer_count * slot_cap,
            bytes_accessed=2 << 20,
            transcendentals=0,
        ),
        name="take_rows",
    )(send_rows.T, send_count[None, :], node_feats)


def shards(
    node_feats,
    weight,
    cotangent,
    degrees,
    local_weights,
    local_tiles,
    send_rows,
    send_count,
    recv_target,
    recv_weight,
):
    row_count, feat_width = node_feats.shape
    tile_size = local_weights.shape[2]
    tile_count = row_count // tile_size
    listed = local_tiles.shape[1]
    peer_count = lax.axis_size(DOM)
    slot_cap = send_rows.shape[1]
    slot_count = peer_count * slot_cap
    nodes_all = row_count * lax.axis_size(DOM + ("slab",))
    column_ids = jnp.arange(tile_count, dtype=jnp.int32)
    selector = (local_tiles[:, :, None] == column_ids[None, None, :]).astype(jnp.bfloat16)
    blocks = local_weights.reshape(tile_count, tile_size, listed, tile_size).astype(jnp.bfloat16)
    adjacency = jnp.einsum("ikj,iakb->iajb", selector, blocks, preferred_element_type=jnp.float32)
    adjacency = adjacency.reshape(row_count, row_count).astype(jnp.bfloat16)
    live_slot = jnp.arange(slot_cap, dtype=jnp.int32)[None, :] < send_count[:, None]
    row_ids = jnp.arange(row_count, dtype=jnp.int32)
    slot_ids = jnp.arange(slot_count, dtype=jnp.int32)
    live_rows = jnp.where(live_slot, send_rows, row_count).astype(jnp.bfloat16)
    to_slot = jnp.arange(peer_count, dtype=jnp.int32)[:, None] == slot_ids[None, :] // slot_cap
    spread = lax.dot_general(
        live_rows,
        to_slot.astype(jnp.bfloat16),
        (((0,), (0,)), ((), ())),
        preferred_element_type=jnp.float32,
    )
    own_column = jnp.arange(slot_cap, dtype=jnp.int32)[:, None] == slot_ids[None, :] % slot_cap
    flat_rows = jnp.sum(jnp.where(own_column, spread, 0.0), axis=0)
    owner = (row_ids[:, None] == flat_rows.astype(jnp.int32)[None, :]).astype(jnp.bfloat16)
    outgoing = take_rows(send_rows, send_count, node_feats)
    outgoing = outgoing.reshape(peer_count, slot_cap, feat_width)
    incoming = lax.all_to_all(outgoing, DOM, split_axis=0, concat_axis=0, tiled=True).reshape(
        slot_count, feat_width
    )
    local_sum = jnp.dot(
        adjacency, node_feats, preferred_element_type=jnp.float32
    ) + node_feats.astype(jnp.float32)
    mixing = jnp.sum(
        jnp.where(row_ids[:, None, None] == recv_target[None, :, :], recv_weight[None, :, :], 0),
        axis=2,
    )
    mixing = mixing.astype(jnp.bfloat16)
    inv_degree = 1.0 / degrees.astype(jnp.float32)
    output, aggregated, grad_pre, grad_sum, slot_grad = layer(
        incoming, mixing, local_sum, inv_degree, weight, cotangent
    )
    slot_grad = slot_grad.reshape(peer_count, slot_cap, feat_width)
    slot_grad, aggregated = lax.optimization_barrier((slot_grad, aggregated))
    returned = lax.all_to_all(slot_grad, DOM, split_axis=0, concat_axis=0, tiled=True)
    returned = returned.reshape(slot_count, feat_width)
    weight_part = lax.dot_general(
        aggregated, grad_pre, (((0,), (0,)), ((), ())), preferred_element_type=jnp.float32
    )
    mine = sum_blocks(weight_part)
    returned, mine = lax.optimization_barrier((returned, mine))
    grad_weight = finish_sum(mine, 1.0 / math.sqrt(nodes_all))
    local_back = lax.dot_general(
        adjacency, grad_sum, (((0,), (0,)), ((), ())), preferred_element_type=jnp.float32
    )
    local_back = local_back + grad_sum.astype(jnp.float32)
    remote_back = jnp.dot(owner, returned, preferred_element_type=jnp.float32)
    grad_feats = (local_back + remote_back).astype(jnp.bfloat16)
    return (output, grad_feats, grad_weight)


def solution(mesh):
    slab_count = mesh.shape["slab"]
    split = Mesh(
        mesh.devices.reshape(4, 4, -1, 2, slab_count), ("y", "z_hi", "z_lo", "core", "slab")
    )
    nodes = P(DOM + ("slab",))
    in_specs = (nodes, P(), nodes, nodes, nodes, nodes, nodes, nodes, nodes, nodes)
    out_specs = (nodes, nodes, P())
    return jax.shard_map(shards, mesh=split, in_specs=in_specs, out_specs=out_specs, check_vma=False)
```

```python
import math

import jax
import jax.numpy as jnp
from jax import lax
from jax.experimental import pallas as pl
from jax.experimental.pallas import tpu as pltpu
from jax.sharding import Mesh
from jax.sharding import PartitionSpec as P


DOM = ("y", "z_hi", "z_lo", "core")


def from_peer(value, axis, mask):
    count = lax.axis_size(axis)
    return lax.ppermute(value, axis, [(place, place ^ mask) for place in range(count)])


def scatter_sum(part, axis, crossing=jnp.bfloat16):
    count, here = lax.axis_size(axis), lax.axis_index(axis)
    rows = part.shape[0] // count
    total = lax.dynamic_slice_in_dim(part, here * rows, rows)
    for mask in range(1, count):
        block = lax.dynamic_slice_in_dim(part, (here ^ mask) * rows, rows)
        total = total + from_peer(block.astype(crossing), axis, mask).astype(jnp.float32)
    return total


def quad_sum(value, axis):
    value = value.astype(jnp.bfloat16)
    near, middle, far = (from_peer(value, axis, mask).astype(jnp.float32) for mask in (1, 2, 3))
    return (value.astype(jnp.float32) + near) + (middle + far)


def to_all(value, axes):
    count = lax.axis_size(axes)
    value = jnp.broadcast_to(value[None], (count,) + value.shape)
    return lax.all_to_all(value, axes, split_axis=0, concat_axis=0, tiled=True)


PLANE = ("core", "slab", "y")


def sum_blocks(part):
    mine = scatter_sum(scatter_sum(scatter_sum(part, "core", jnp.float32), "slab"), "y")
    return quad_sum(mine, "z_hi")


def finish_sum(mine, scale):
    mine = (jnp.sum(to_all(mine, "z_lo"), axis=0) * scale).astype(jnp.bfloat16)
    return to_all(mine, PLANE).reshape(-1, mine.shape[-1]).astype(jnp.float32)


VMEM = pl.BlockSpec(memory_space=pltpu.VMEM)
HBM = pl.BlockSpec(memory_space=pltpu.HBM)
PARTS = 4


def layer_kernel(
    incoming, mixing, mixing_rows, local_sum, inv_degree, weight, cotangent,
    output, aggregated, grad_pre, grad_sum, slot_grad,
    output_rows, aggregated_rows, grad_rows, summed_rows, slots, done,
):
    copies = []

    def leave(source, target):
        copy = pltpu.make_async_copy(source, target, done.at[len(copies)])
        copy.start()
        copies.append(copy)

    inverse = inv_degree[...]
    remote = jnp.dot(mixing[...], incoming[...], preferred_element_type=jnp.float32)
    gathered = ((local_sum[...] + remote) * inverse).astype(jnp.bfloat16)
    aggregated_rows[...] = gathered
    leave(aggregated_rows, aggregated)
    pre_act = jnp.dot(gathered, weight[...], preferred_element_type=jnp.float32)
    gating_value = jax.nn.sigmoid(pre_act)
    output_rows[...] = (pre_act * gating_value).astype(jnp.bfloat16)
    leave(output_rows, output)
    scaled = cotangent[...].astype(jnp.float32) * gating_value
    grad = (scaled * (1.0 + pre_act * (1.0 - gating_value))).astype(jnp.bfloat16)
    grad_rows[...] = grad
    leave(grad_rows, grad_pre)
    summed = lax.dot_general(
        grad, weight[...], (((1,), (1,)), ((), ())), preferred_element_type=jnp.float32
    )
    summed = (summed * inverse).astype(jnp.bfloat16)
    summed_rows[...] = summed
    leave(summed_rows, grad_sum)
    rows = slots.shape[0] // PARTS
    for part in range(PARTS):
        span = pl.ds(part * rows, rows)
        slots[span, :] = jnp.dot(
            mixing_rows[span, :], summed, preferred_element_type=jnp.float32
        ).astype(jnp.bfloat16)
        leave(slots.at[span, :], slot_grad.at[span, :])
    for copy in copies:
        copy.wait()


def layer(incoming, mixing, local_sum, inv_degree, weight, cotangent):
    nodes, slot_count = mixing.shape
    width = weight.shape[0]
    rows = pltpu.HBM((nodes, width), jnp.bfloat16)
    return pl.pallas_call(
        layer_kernel,
        out_shape=(rows, rows, rows, rows, pltpu.HBM((slot_count, width), jnp.bfloat16)),
        in_specs=[VMEM] * 7,
        out_specs=(HBM,) * 5,
        scratch_shapes=[pltpu.VMEM((nodes, width), jnp.bfloat16)] * 4
        + [
            pltpu.VMEM((slot_count, width), jnp.bfloat16),
            pltpu.SemaphoreType.DMA((4 + PARTS,)),
        ],
        compiler_params=pltpu.CompilerParams(vmem_limit_bytes=24 << 20),
        cost_estimate=pl.CostEstimate(
            flops=2 * nodes * width * (2 * slot_count + 2 * width),
            bytes_accessed=6 << 20,
            transcendentals=nodes * width,
        ),
        name="layer",
    )(incoming, mixing, mixing.T, local_sum, inv_degree[:, None], weight, cotangent)


def take_kernel(
    send_rows, send_count, node_feats, outgoing, row_table, counts, feats, taken, ready, done
):
    arrivals = []
    for at, (source, target) in enumerate(
        ((send_rows, row_table), (send_count, counts), (node_feats, feats))
    ):
        copy = pltpu.make_async_copy(source, target, ready.at[at])
        copy.start()
        arrivals.append(copy)
    slot_cap, peer_count = row_table.shape
    nodes, slot_count = feats.shape[0], taken.shape[0]
    slot = lax.broadcasted_iota(jnp.int32, (slot_count, peer_count), 0)
    first = slot_cap * lax.broadcasted_iota(jnp.int32, (slot_count, peer_count), 1)
    place = jnp.where((slot >= first) & (slot < first + slot_cap), 1.0, 0.0)
    slot = lax.broadcasted_iota(jnp.int32, (slot_count, slot_cap), 0)
    column = lax.rem(slot, slot_cap) == lax.broadcasted_iota(jnp.int32, slot.shape, 1)
    arrivals[0].wait()
    arrivals[1].wait()
    rank = lax.broadcasted_iota(jnp.int32, (slot_cap, peer_count), 0)
    live = jnp.where(rank < counts[...], row_table[...], nodes).astype(jnp.float32)
    spread = lax.dot_general(
        place.astype(jnp.bfloat16),
        live.astype(jnp.bfloat16),
        (((1,), (1,)), ((), ())),
        preferred_element_type=jnp.float32,
    )
    spread = jnp.where(column, spread, 0.0).astype(jnp.bfloat16)
    row = jnp.dot(
        spread, jnp.ones((slot_cap, nodes), jnp.bfloat16), preferred_element_type=jnp.float32
    )
    node = lax.broadcasted_iota(jnp.int32, row.shape, 1).astype(jnp.float32)
    chosen = jnp.where(row == node, 1.0, 0.0).astype(jnp.bfloat16)
    arrivals[2].wait()
    rows = slot_count // PARTS
    copies = []
    for part in range(PARTS):
        span = pl.ds(part * rows, rows)
        taken[span, :] = jnp.dot(
            chosen[part * rows : (part + 1) * rows], feats[...], preferred_element_type=jnp.float32
        ).astype(jnp.bfloat16)
        copy = pltpu.make_async_copy(taken.at[span, :], outgoing.at[span, :], done.at[part])
        copy.start()
        copies.append(copy)
    for copy in copies:
        copy.wait()


def take_rows(send_rows, send_count, node_feats):
    peer_count, slot_cap = send_rows.shape
    nodes, width = node_feats.shape
    slots = jax.ShapeDtypeStruct((peer_count * slot_cap, width), jnp.bfloat16)
    return pl.pallas_call(
        take_kernel,
        out_shape=slots,
        in_specs=[HBM] * 3,
        out_specs=HBM,
        scratch_shapes=[
            pltpu.VMEM((slot_cap, peer_count), jnp.int32),
            pltpu.VMEM((1, peer_count), jnp.int32),
            pltpu.VMEM((nodes, width), jnp.bfloat16),
            pltpu.VMEM(slots.shape, slots.dtype),
            pltpu.SemaphoreType.DMA((3,)),
            pltpu.SemaphoreType.DMA((PARTS,)),
        ],
        compiler_params=pltpu.CompilerParams(vmem_limit_bytes=63_400_000),
        cost_estimate=pl.CostEstimate(
            flops=2 * nodes * width * peer_count * slot_cap,
            bytes_accessed=2 << 20,
            transcendentals=0,
        ),
        name="take_rows",
    )(send_rows.T, send_count[None, :], node_feats)


def shards(
    node_feats,
    weight,
    cotangent,
    degrees,
    local_weights,
    local_tiles,
    send_rows,
    send_count,
    recv_target,
    recv_weight,
):
    row_count, feat_width = node_feats.shape
    tile_size = local_weights.shape[2]
    tile_count = row_count // tile_size
    listed = local_tiles.shape[1]
    peer_count = lax.axis_size(DOM)
    slot_cap = send_rows.shape[1]
    slot_count = peer_count * slot_cap
    nodes_all = row_count * lax.axis_size(DOM + ("slab",))
    column_ids = jnp.arange(tile_count, dtype=jnp.int32)
    selector = (local_tiles[:, :, None] == column_ids[None, None, :]).astype(jnp.bfloat16)
    blocks = local_weights.reshape(tile_count, tile_size, listed, tile_size).astype(jnp.bfloat16)
    adjacency = jnp.einsum("ikj,iakb->iajb", selector, blocks, preferred_element_type=jnp.float32)
    adjacency = adjacency.reshape(row_count, row_count).astype(jnp.bfloat16)
    live_slot = jnp.arange(slot_cap, dtype=jnp.int32)[None, :] < send_count[:, None]
    row_ids = jnp.arange(row_count, dtype=jnp.int32)
    slot_ids = jnp.arange(slot_count, dtype=jnp.int32)
    live_rows = jnp.where(live_slot, send_rows, row_count).astype(jnp.bfloat16)
    to_slot = jnp.arange(peer_count, dtype=jnp.int32)[:, None] == slot_ids[None, :] // slot_cap
    spread = lax.dot_general(
        live_rows,
        to_slot.astype(jnp.bfloat16),
        (((0,), (0,)), ((), ())),
        preferred_element_type=jnp.float32,
    )
    own_column = jnp.arange(slot_cap, dtype=jnp.int32)[:, None] == slot_ids[None, :] % slot_cap
    flat_rows = jnp.sum(jnp.where(own_column, spread, 0.0), axis=0)
    owner = (row_ids[:, None] == flat_rows.astype(jnp.int32)[None, :]).astype(jnp.bfloat16)
    outgoing = take_rows(send_rows, send_count, node_feats)
    outgoing = outgoing.reshape(peer_count, slot_cap, feat_width)
    incoming = lax.all_to_all(outgoing, DOM, split_axis=0, concat_axis=0, tiled=True).reshape(
        slot_count, feat_width
    )
    local_sum = jnp.dot(
        adjacency, node_feats, preferred_element_type=jnp.float32
    ) + node_feats.astype(jnp.float32)
    mixing = jnp.sum(
        jnp.where(row_ids[:, None, None] == recv_target[None, :, :], recv_weight[None, :, :], 0),
        axis=2,
    )
    mixing = mixing.astype(jnp.bfloat16)
    inv_degree = 1.0 / degrees.astype(jnp.float32)
    output, aggregated, grad_pre, grad_sum, slot_grad = layer(
        incoming, mixing, local_sum, inv_degree, weight, cotangent
    )
    slot_grad = slot_grad.reshape(peer_count, slot_cap, feat_width)
    slot_grad, aggregated = lax.optimization_barrier((slot_grad, aggregated))
    returned = lax.all_to_all(slot_grad, DOM, split_axis=0, concat_axis=0, tiled=True)
    returned = returned.reshape(slot_count, feat_width)
    weight_part = lax.dot_general(
        aggregated, grad_pre, (((0,), (0,)), ((), ())), preferred_element_type=jnp.float32
    )
    mine = sum_blocks(weight_part)
    returned, mine = lax.optimization_barrier((returned, mine))
    grad_weight = finish_sum(mine, 1.0 / math.sqrt(nodes_all))
    local_back = lax.dot_general(
        adjacency, grad_sum, (((0,), (0,)), ((), ())), preferred_element_type=jnp.float32
    )
    local_back = local_back + grad_sum.astype(jnp.float32)
    remote_back = jnp.dot(owner, returned, preferred_element_type=jnp.float32)
    grad_feats = (local_back + remote_back).astype(jnp.bfloat16)
    return (output, grad_feats, grad_weight)


def solution(mesh):
    slab_count = mesh.shape["slab"]
    split = Mesh(
        mesh.devices.reshape(4, 4, -1, 2, slab_count), ("y", "z_hi", "z_lo", "core", "slab")
    )
    nodes = P(DOM + ("slab",))
    in_specs = (nodes, P(), nodes, nodes, nodes, nodes, nodes, nodes, nodes, nodes)
    out_specs = (nodes, nodes, P())
    return jax.shard_map(shards, mesh=split, in_specs=in_specs, out_specs=out_specs, check_vma=False)
```

```python
import math

import jax
import jax.numpy as jnp
from jax import lax
from jax.experimental import pallas as pl
from jax.experimental.pallas import tpu as pltpu
from jax.sharding import Mesh
from jax.sharding import PartitionSpec as P


DOM = ("y", "z_hi", "z_lo", "core")


def from_peer(value, axis, mask):
    count = lax.axis_size(axis)
    return lax.ppermute(value, axis, [(place, place ^ mask) for place in range(count)])


def scatter_sum(part, axis, crossing=jnp.bfloat16):
    count, here = lax.axis_size(axis), lax.axis_index(axis)
    rows = part.shape[0] // count
    total = lax.dynamic_slice_in_dim(part, here * rows, rows)
    for mask in range(1, count):
        block = lax.dynamic_slice_in_dim(part, (here ^ mask) * rows, rows)
        total = total + from_peer(block.astype(crossing), axis, mask).astype(jnp.float32)
    return total


def quad_sum(value, axis):
    value = value.astype(jnp.bfloat16)
    near, middle, far = (from_peer(value, axis, mask).astype(jnp.float32) for mask in (1, 2, 3))
    return (value.astype(jnp.float32) + near) + (middle + far)


def to_all(value, axes):
    count = lax.axis_size(axes)
    value = jnp.broadcast_to(value[None], (count,) + value.shape)
    return lax.all_to_all(value, axes, split_axis=0, concat_axis=0, tiled=True)


PLANE = ("core", "slab", "y")


def sum_blocks(part):
    mine = scatter_sum(scatter_sum(scatter_sum(part, "core", jnp.float32), "slab"), "y", jnp.float32)
    return quad_sum(mine, "z_hi")


def finish_sum(mine, scale):
    mine = (jnp.sum(to_all(mine.astype(jnp.bfloat16), "z_lo").astype(jnp.float32), axis=0) * scale).astype(jnp.bfloat16)
    return to_all(mine, PLANE).reshape(-1, mine.shape[-1]).astype(jnp.float32)


VMEM = pl.BlockSpec(memory_space=pltpu.VMEM)
HBM = pl.BlockSpec(memory_space=pltpu.HBM)
PARTS = 4


def layer_kernel(
    incoming, mixing, mixing_rows, local_sum, inv_degree, weight, cotangent,
    output, aggregated, grad_pre, grad_sum, slot_grad,
    output_rows, aggregated_rows, grad_rows, summed_rows, slots, done,
):
    copies = []

    def leave(source, target):
        copy = pltpu.make_async_copy(source, target, done.at[len(copies)])
        copy.start()
        copies.append(copy)

    inverse = inv_degree[...]
    remote = jnp.dot(mixing[...], incoming[...], preferred_element_type=jnp.float32)
    gathered = ((local_sum[...] + remote) * inverse).astype(jnp.bfloat16)
    aggregated_rows[...] = gathered
    leave(aggregated_rows, aggregated)
    pre_act = jnp.dot(gathered, weight[...], preferred_element_type=jnp.float32)
    gating_value = jax.nn.sigmoid(pre_act)
    output_rows[...] = (pre_act * gating_value).astype(jnp.bfloat16)
    leave(output_rows, output)
    scaled = cotangent[...].astype(jnp.float32) * gating_value
    grad = (scaled * (1.0 + pre_act * (1.0 - gating_value))).astype(jnp.bfloat16)
    grad_rows[...] = grad
    leave(grad_rows, grad_pre)
    summed = lax.dot_general(
        grad, weight[...], (((1,), (1,)), ((), ())), preferred_element_type=jnp.float32
    )
    summed = (summed * inverse).astype(jnp.bfloat16)
    summed_rows[...] = summed
    leave(summed_rows, grad_sum)
    rows = slots.shape[0] // PARTS
    for part in range(PARTS):
        span = pl.ds(part * rows, rows)
        slots[span, :] = jnp.dot(
            mixing_rows[span, :], summed, preferred_element_type=jnp.float32
        ).astype(jnp.bfloat16)
        leave(slots.at[span, :], slot_grad.at[span, :])
    for copy in copies:
        copy.wait()


def layer(incoming, mixing, local_sum, inv_degree, weight, cotangent):
    nodes, slot_count = mixing.shape
    width = weight.shape[0]
    rows = pltpu.HBM((nodes, width), jnp.bfloat16)
    return pl.pallas_call(
        layer_kernel,
        out_shape=(rows, rows, rows, rows, pltpu.HBM((slot_count, width), jnp.bfloat16)),
        in_specs=[VMEM] * 7,
        out_specs=(HBM,) * 5,
        scratch_shapes=[pltpu.VMEM((nodes, width), jnp.bfloat16)] * 4
        + [
            pltpu.VMEM((slot_count, width), jnp.bfloat16),
            pltpu.SemaphoreType.DMA((4 + PARTS,)),
        ],
        compiler_params=pltpu.CompilerParams(vmem_limit_bytes=24 << 20),
        cost_estimate=pl.CostEstimate(
            flops=2 * nodes * width * (2 * slot_count + 2 * width),
            bytes_accessed=6 << 20,
            transcendentals=nodes * width,
        ),
        name="layer",
    )(incoming, mixing, mixing.T, local_sum, inv_degree[:, None], weight, cotangent)


def take_kernel(
    send_rows, send_count, node_feats, outgoing, row_table, counts, feats, taken, ready, done
):
    arrivals = []
    for at, (source, target) in enumerate(
        ((send_rows, row_table), (send_count, counts), (node_feats, feats))
    ):
        copy = pltpu.make_async_copy(source, target, ready.at[at])
        copy.start()
        arrivals.append(copy)
    slot_cap, peer_count = row_table.shape
    nodes, slot_count = feats.shape[0], taken.shape[0]
    slot = lax.broadcasted_iota(jnp.int32, (slot_count, peer_count), 0)
    first = slot_cap * lax.broadcasted_iota(jnp.int32, (slot_count, peer_count), 1)
    place = jnp.where((slot >= first) & (slot < first + slot_cap), 1.0, 0.0)
    slot = lax.broadcasted_iota(jnp.int32, (slot_count, slot_cap), 0)
    column = lax.rem(slot, slot_cap) == lax.broadcasted_iota(jnp.int32, slot.shape, 1)
    arrivals[0].wait()
    arrivals[1].wait()
    rank = lax.broadcasted_iota(jnp.int32, (slot_cap, peer_count), 0)
    live = jnp.where(rank < counts[...], row_table[...], nodes).astype(jnp.float32)
    spread = lax.dot_general(
        place.astype(jnp.bfloat16),
        live.astype(jnp.bfloat16),
        (((1,), (1,)), ((), ())),
        preferred_element_type=jnp.float32,
    )
    spread = jnp.where(column, spread, 0.0).astype(jnp.bfloat16)
    row = jnp.dot(
        spread, jnp.ones((slot_cap, nodes), jnp.bfloat16), preferred_element_type=jnp.float32
    )
    node = lax.broadcasted_iota(jnp.int32, row.shape, 1).astype(jnp.float32)
    chosen = jnp.where(row == node, 1.0, 0.0).astype(jnp.bfloat16)
    arrivals[2].wait()
    rows = slot_count // PARTS
    copies = []
    for part in range(PARTS):
        span = pl.ds(part * rows, rows)
        taken[span, :] = jnp.dot(
            chosen[part * rows : (part + 1) * rows], feats[...], preferred_element_type=jnp.float32
        ).astype(jnp.bfloat16)
        copy = pltpu.make_async_copy(taken.at[span, :], outgoing.at[span, :], done.at[part])
        copy.start()
        copies.append(copy)
    for copy in copies:
        copy.wait()


def take_rows(send_rows, send_count, node_feats):
    peer_count, slot_cap = send_rows.shape
    nodes, width = node_feats.shape
    slots = jax.ShapeDtypeStruct((peer_count * slot_cap, width), jnp.bfloat16)
    return pl.pallas_call(
        take_kernel,
        out_shape=slots,
        in_specs=[HBM] * 3,
        out_specs=HBM,
        scratch_shapes=[
            pltpu.VMEM((slot_cap, peer_count), jnp.int32),
            pltpu.VMEM((1, peer_count), jnp.int32),
            pltpu.VMEM((nodes, width), jnp.bfloat16),
            pltpu.VMEM(slots.shape, slots.dtype),
            pltpu.SemaphoreType.DMA((3,)),
            pltpu.SemaphoreType.DMA((PARTS,)),
        ],
        compiler_params=pltpu.CompilerParams(vmem_limit_bytes=63_400_000),
        cost_estimate=pl.CostEstimate(
            flops=2 * nodes * width * peer_count * slot_cap,
            bytes_accessed=2 << 20,
            transcendentals=0,
        ),
        name="take_rows",
    )(send_rows.T, send_count[None, :], node_feats)


def shards(
    node_feats,
    weight,
    cotangent,
    degrees,
    local_weights,
    local_tiles,
    send_rows,
    send_count,
    recv_target,
    recv_weight,
):
    row_count, feat_width = node_feats.shape
    tile_size = local_weights.shape[2]
    tile_count = row_count // tile_size
    listed = local_tiles.shape[1]
    peer_count = lax.axis_size(DOM)
    slot_cap = send_rows.shape[1]
    slot_count = peer_count * slot_cap
    nodes_all = row_count * lax.axis_size(DOM + ("slab",))
    column_ids = jnp.arange(tile_count, dtype=jnp.int32)
    selector = (local_tiles[:, :, None] == column_ids[None, None, :]).astype(jnp.bfloat16)
    blocks = local_weights.reshape(tile_count, tile_size, listed, tile_size).astype(jnp.bfloat16)
    adjacency = jnp.einsum("ikj,iakb->iajb", selector, blocks, preferred_element_type=jnp.float32)
    adjacency = adjacency.reshape(row_count, row_count).astype(jnp.bfloat16)
    live_slot = jnp.arange(slot_cap, dtype=jnp.int32)[None, :] < send_count[:, None]
    row_ids = jnp.arange(row_count, dtype=jnp.int32)
    slot_ids = jnp.arange(slot_count, dtype=jnp.int32)
    live_rows = jnp.where(live_slot, send_rows, row_count).astype(jnp.bfloat16)
    to_slot = jnp.arange(peer_count, dtype=jnp.int32)[:, None] == slot_ids[None, :] // slot_cap
    spread = lax.dot_general(
        live_rows,
        to_slot.astype(jnp.bfloat16),
        (((0,), (0,)), ((), ())),
        preferred_element_type=jnp.float32,
    )
    own_column = jnp.arange(slot_cap, dtype=jnp.int32)[:, None] == slot_ids[None, :] % slot_cap
    flat_rows = jnp.sum(jnp.where(own_column, spread, 0.0), axis=0)
    owner = (row_ids[:, None] == flat_rows.astype(jnp.int32)[None, :]).astype(jnp.bfloat16)
    outgoing = take_rows(send_rows, send_count, node_feats)
    outgoing = outgoing.reshape(peer_count, slot_cap, feat_width)
    incoming = lax.all_to_all(outgoing, DOM, split_axis=0, concat_axis=0, tiled=True).reshape(
        slot_count, feat_width
    )
    local_sum = jnp.dot(
        adjacency, node_feats, preferred_element_type=jnp.float32
    ) + node_feats.astype(jnp.float32)
    mixing = jnp.sum(
        jnp.where(row_ids[:, None, None] == recv_target[None, :, :], recv_weight[None, :, :], 0),
        axis=2,
    )
    mixing = mixing.astype(jnp.bfloat16)
    inv_degree = 1.0 / degrees.astype(jnp.float32)
    output, aggregated, grad_pre, grad_sum, slot_grad = layer(
        incoming, mixing, local_sum, inv_degree, weight, cotangent
    )
    slot_grad = slot_grad.reshape(peer_count, slot_cap, feat_width)
    slot_grad, aggregated = lax.optimization_barrier((slot_grad, aggregated))
    returned = lax.all_to_all(slot_grad, DOM, split_axis=0, concat_axis=0, tiled=True)
    returned = returned.reshape(slot_count, feat_width)
    weight_part = lax.dot_general(
        aggregated, grad_pre, (((0,), (0,)), ((), ())), preferred_element_type=jnp.float32
    )
    mine = sum_blocks(weight_part)
    returned, mine = lax.optimization_barrier((returned, mine))
    grad_weight = finish_sum(mine, 1.0 / math.sqrt(nodes_all))
    local_back = lax.dot_general(
        adjacency, grad_sum, (((0,), (0,)), ((), ())), preferred_element_type=jnp.float32
    )
    local_back = local_back + grad_sum.astype(jnp.float32)
    remote_back = jnp.dot(owner, returned, preferred_element_type=jnp.float32)
    grad_feats = (local_back + remote_back).astype(jnp.bfloat16)
    return (output, grad_feats, grad_weight)


def solution(mesh):
    slab_count = mesh.shape["slab"]
    split = Mesh(
        mesh.devices.reshape(4, 4, -1, 2, slab_count), ("y", "z_hi", "z_lo", "core", "slab")
    )
    nodes = P(DOM + ("slab",))
    in_specs = (nodes, P(), nodes, nodes, nodes, nodes, nodes, nodes, nodes, nodes)
    out_specs = (nodes, nodes, P())
    return jax.shard_map(shards, mesh=split, in_specs=in_specs, out_specs=out_specs, check_vma=False)
```

```python
import math

import jax
import jax.numpy as jnp
from jax import lax
from jax.experimental import pallas as pl
from jax.experimental.pallas import tpu as pltpu
from jax.sharding import Mesh
from jax.sharding import PartitionSpec as P


DOM = ("y", "z_hi", "z_lo", "core")


def from_peer(value, axis, mask):
    count = lax.axis_size(axis)
    return lax.ppermute(value, axis, [(place, place ^ mask) for place in range(count)])


def scatter_sum(part, axis, crossing=jnp.bfloat16):
    count, here = lax.axis_size(axis), lax.axis_index(axis)
    rows = part.shape[0] // count
    total = lax.dynamic_slice_in_dim(part, here * rows, rows)
    for mask in range(1, count):
        block = lax.dynamic_slice_in_dim(part, (here ^ mask) * rows, rows)
        total = total + from_peer(block.astype(crossing), axis, mask).astype(jnp.float32)
    return total


def quad_sum(value, axis):
    value = value.astype(jnp.bfloat16)
    near, middle, far = (from_peer(value, axis, mask).astype(jnp.float32) for mask in (1, 2, 3))
    return (value.astype(jnp.float32) + near) + (middle + far)


def to_all(value, axes):
    count = lax.axis_size(axes)
    value = jnp.broadcast_to(value[None], (count,) + value.shape)
    return lax.all_to_all(value, axes, split_axis=0, concat_axis=0, tiled=True)


def sum_blocks(part):
    rows, width = part.shape
    plane, cores = lax.axis_size(("slab", "y")), lax.axis_size("core")
    part = part.reshape(plane, cores, rows // plane // cores, width).swapaxes(0, 1)
    mine = scatter_sum(part.reshape(rows, width), "core", jnp.float32)
    return quad_sum(scatter_sum(scatter_sum(mine, "slab"), "y", jnp.float32), "z_hi")


def finish_sum(mine, scale):
    quads = to_all(mine.astype(jnp.bfloat16), ("core", "z_lo"))
    quads = quads.reshape((lax.axis_size("core"), lax.axis_size("z_lo")) + mine.shape)
    mine = (jnp.sum(quads.astype(jnp.float32), axis=1) * scale).astype(jnp.bfloat16)
    mine = mine.reshape(-1, mine.shape[-1])
    return to_all(mine, ("slab", "y")).reshape(-1, mine.shape[-1]).astype(jnp.float32)


VMEM = pl.BlockSpec(memory_space=pltpu.VMEM)
HBM = pl.BlockSpec(memory_space=pltpu.HBM)
PARTS = 4


def layer_kernel(
    incoming, mixing, mixing_rows, local_sum, inv_degree, weight, cotangent,
    output, aggregated, grad_pre, grad_sum, slot_grad,
    output_rows, aggregated_rows, grad_rows, summed_rows, slots, done,
):
    copies = []

    def leave(source, target):
        copy = pltpu.make_async_copy(source, target, done.at[len(copies)])
        copy.start()
        copies.append(copy)

    inverse = inv_degree[...]
    remote = jnp.dot(mixing[...], incoming[...], preferred_element_type=jnp.float32)
    gathered = ((local_sum[...] + remote) * inverse).astype(jnp.bfloat16)
    aggregated_rows[...] = gathered
    leave(aggregated_rows, aggregated)
    pre_act = jnp.dot(gathered, weight[...], preferred_element_type=jnp.float32)
    gating_value = jax.nn.sigmoid(pre_act)
    output_rows[...] = (pre_act * gating_value).astype(jnp.bfloat16)
    leave(output_rows, output)
    scaled = cotangent[...].astype(jnp.float32) * gating_value
    grad = (scaled * (1.0 + pre_act * (1.0 - gating_value))).astype(jnp.bfloat16)
    grad_rows[...] = grad
    leave(grad_rows, grad_pre)
    summed = lax.dot_general(
        grad, weight[...], (((1,), (1,)), ((), ())), preferred_element_type=jnp.float32
    )
    summed = (summed * inverse).astype(jnp.bfloat16)
    summed_rows[...] = summed
    leave(summed_rows, grad_sum)
    rows = slots.shape[0] // PARTS
    for part in range(PARTS):
        span = pl.ds(part * rows, rows)
        slots[span, :] = jnp.dot(
            mixing_rows[span, :], summed, preferred_element_type=jnp.float32
        ).astype(jnp.bfloat16)
        leave(slots.at[span, :], slot_grad.at[span, :])
    for copy in copies:
        copy.wait()


def layer(incoming, mixing, local_sum, inv_degree, weight, cotangent):
    nodes, slot_count = mixing.shape
    width = weight.shape[0]
    rows = pltpu.HBM((nodes, width), jnp.bfloat16)
    return pl.pallas_call(
        layer_kernel,
        out_shape=(rows, rows, rows, rows, pltpu.HBM((slot_count, width), jnp.bfloat16)),
        in_specs=[VMEM] * 7,
        out_specs=(HBM,) * 5,
        scratch_shapes=[pltpu.VMEM((nodes, width), jnp.bfloat16)] * 4
        + [
            pltpu.VMEM((slot_count, width), jnp.bfloat16),
            pltpu.SemaphoreType.DMA((4 + PARTS,)),
        ],
        compiler_params=pltpu.CompilerParams(vmem_limit_bytes=24 << 20),
        cost_estimate=pl.CostEstimate(
            flops=2 * nodes * width * (2 * slot_count + 2 * width),
            bytes_accessed=6 << 20,
            transcendentals=nodes * width,
        ),
        name="layer",
    )(incoming, mixing, mixing.T, local_sum, inv_degree[:, None], weight, cotangent)


def take_kernel(
    send_rows, send_count, node_feats, outgoing, row_table, counts, feats, taken, ready, done
):
    arrivals = []
    for at, (source, target) in enumerate(
        ((send_rows, row_table), (send_count, counts), (node_feats, feats))
    ):
        copy = pltpu.make_async_copy(source, target, ready.at[at])
        copy.start()
        arrivals.append(copy)
    slot_cap, peer_count = row_table.shape
    nodes, slot_count = feats.shape[0], taken.shape[0]
    slot = lax.broadcasted_iota(jnp.int32, (slot_count, peer_count), 0)
    first = slot_cap * lax.broadcasted_iota(jnp.int32, (slot_count, peer_count), 1)
    place = jnp.where((slot >= first) & (slot < first + slot_cap), 1.0, 0.0)
    slot = lax.broadcasted_iota(jnp.int32, (slot_count, slot_cap), 0)
    column = lax.rem(slot, slot_cap) == lax.broadcasted_iota(jnp.int32, slot.shape, 1)
    arrivals[0].wait()
    arrivals[1].wait()
    rank = lax.broadcasted_iota(jnp.int32, (slot_cap, peer_count), 0)
    live = jnp.where(rank < counts[...], row_table[...], nodes).astype(jnp.float32)
    spread = lax.dot_general(
        place.astype(jnp.bfloat16),
        live.astype(jnp.bfloat16),
        (((1,), (1,)), ((), ())),
        preferred_element_type=jnp.float32,
    )
    spread = jnp.where(column, spread, 0.0).astype(jnp.bfloat16)
    row = jnp.dot(
        spread, jnp.ones((slot_cap, nodes), jnp.bfloat16), preferred_element_type=jnp.float32
    )
    node = lax.broadcasted_iota(jnp.int32, row.shape, 1).astype(jnp.float32)
    chosen = jnp.where(row == node, 1.0, 0.0).astype(jnp.bfloat16)
    arrivals[2].wait()
    rows = slot_count // PARTS
    copies = []
    for part in range(PARTS):
        span = pl.ds(part * rows, rows)
        taken[span, :] = jnp.dot(
            chosen[part * rows : (part + 1) * rows], feats[...], preferred_element_type=jnp.float32
        ).astype(jnp.bfloat16)
        copy = pltpu.make_async_copy(taken.at[span, :], outgoing.at[span, :], done.at[part])
        copy.start()
        copies.append(copy)
    for copy in copies:
        copy.wait()


def take_rows(send_rows, send_count, node_feats):
    peer_count, slot_cap = send_rows.shape
    nodes, width = node_feats.shape
    slots = jax.ShapeDtypeStruct((peer_count * slot_cap, width), jnp.bfloat16)
    return pl.pallas_call(
        take_kernel,
        out_shape=slots,
        in_specs=[HBM] * 3,
        out_specs=HBM,
        scratch_shapes=[
            pltpu.VMEM((slot_cap, peer_count), jnp.int32),
            pltpu.VMEM((1, peer_count), jnp.int32),
            pltpu.VMEM((nodes, width), jnp.bfloat16),
            pltpu.VMEM(slots.shape, slots.dtype),
            pltpu.SemaphoreType.DMA((3,)),
            pltpu.SemaphoreType.DMA((PARTS,)),
        ],
        compiler_params=pltpu.CompilerParams(vmem_limit_bytes=63_400_000),
        cost_estimate=pl.CostEstimate(
            flops=2 * nodes * width * peer_count * slot_cap,
            bytes_accessed=2 << 20,
            transcendentals=0,
        ),
        name="take_rows",
    )(send_rows.T, send_count[None, :], node_feats)


def shards(
    node_feats,
    weight,
    cotangent,
    degrees,
    local_weights,
    local_tiles,
    send_rows,
    send_count,
    recv_target,
    recv_weight,
):
    row_count, feat_width = node_feats.shape
    tile_size = local_weights.shape[2]
    tile_count = row_count // tile_size
    listed = local_tiles.shape[1]
    peer_count = lax.axis_size(DOM)
    slot_cap = send_rows.shape[1]
    slot_count = peer_count * slot_cap
    nodes_all = row_count * lax.axis_size(DOM + ("slab",))
    column_ids = jnp.arange(tile_count, dtype=jnp.int32)
    selector = (local_tiles[:, :, None] == column_ids[None, None, :]).astype(jnp.bfloat16)
    blocks = local_weights.reshape(tile_count, tile_size, listed, tile_size).astype(jnp.bfloat16)
    adjacency = jnp.einsum("ikj,iakb->iajb", selector, blocks, preferred_element_type=jnp.float32)
    adjacency = adjacency.reshape(row_count, row_count).astype(jnp.bfloat16)
    live_slot = jnp.arange(slot_cap, dtype=jnp.int32)[None, :] < send_count[:, None]
    row_ids = jnp.arange(row_count, dtype=jnp.int32)
    slot_ids = jnp.arange(slot_count, dtype=jnp.int32)
    live_rows = jnp.where(live_slot, send_rows, row_count).astype(jnp.bfloat16)
    to_slot = jnp.arange(peer_count, dtype=jnp.int32)[:, None] == slot_ids[None, :] // slot_cap
    spread = lax.dot_general(
        live_rows,
        to_slot.astype(jnp.bfloat16),
        (((0,), (0,)), ((), ())),
        preferred_element_type=jnp.float32,
    )
    own_column = jnp.arange(slot_cap, dtype=jnp.int32)[:, None] == slot_ids[None, :] % slot_cap
    flat_rows = jnp.sum(jnp.where(own_column, spread, 0.0), axis=0)
    owner = (row_ids[:, None] == flat_rows.astype(jnp.int32)[None, :]).astype(jnp.bfloat16)
    outgoing = take_rows(send_rows, send_count, node_feats)
    outgoing = outgoing.reshape(peer_count, slot_cap, feat_width)
    incoming = lax.all_to_all(outgoing, DOM, split_axis=0, concat_axis=0, tiled=True).reshape(
        slot_count, feat_width
    )
    local_sum = jnp.dot(
        adjacency, node_feats, preferred_element_type=jnp.float32
    ) + node_feats.astype(jnp.float32)
    mixing = jnp.sum(
        jnp.where(row_ids[:, None, None] == recv_target[None, :, :], recv_weight[None, :, :], 0),
        axis=2,
    )
    mixing = mixing.astype(jnp.bfloat16)
    inv_degree = 1.0 / degrees.astype(jnp.float32)
    output, aggregated, grad_pre, grad_sum, slot_grad = layer(
        incoming, mixing, local_sum, inv_degree, weight, cotangent
    )
    slot_grad = slot_grad.reshape(peer_count, slot_cap, feat_width)
    slot_grad, aggregated = lax.optimization_barrier((slot_grad, aggregated))
    returned = lax.all_to_all(slot_grad, DOM, split_axis=0, concat_axis=0, tiled=True)
    returned = returned.reshape(slot_count, feat_width)
    weight_part = lax.dot_general(
        aggregated, grad_pre, (((0,), (0,)), ((), ())), preferred_element_type=jnp.float32
    )
    mine = sum_blocks(weight_part)
    returned, mine = lax.optimization_barrier((returned, mine))
    grad_weight = finish_sum(mine, 1.0 / math.sqrt(nodes_all))
    local_back = lax.dot_general(
        adjacency, grad_sum, (((0,), (0,)), ((), ())), preferred_element_type=jnp.float32
    )
    local_back = local_back + grad_sum.astype(jnp.float32)
    remote_back = jnp.dot(owner, returned, preferred_element_type=jnp.float32)
    grad_feats = (local_back + remote_back).astype(jnp.bfloat16)
    return (output, grad_feats, grad_weight)


def solution(mesh):
    slab_count = mesh.shape["slab"]
    split = Mesh(
        mesh.devices.reshape(4, 4, -1, 2, slab_count), ("y", "z_hi", "z_lo", "core", "slab")
    )
    nodes = P(DOM + ("slab",))
    in_specs = (nodes, P(), nodes, nodes, nodes, nodes, nodes, nodes, nodes, nodes)
    out_specs = (nodes, nodes, P())
    return jax.shard_map(shards, mesh=split, in_specs=in_specs, out_specs=out_specs, check_vma=False)
```

```python
import math

import jax
import jax.numpy as jnp
from jax import lax
from jax.experimental import pallas as pl
from jax.experimental.pallas import tpu as pltpu
from jax.sharding import Mesh
from jax.sharding import PartitionSpec as P


DOM = ("y", "z_hi", "z_lo", "core")


def from_peer(value, axis, mask):
    count = lax.axis_size(axis)
    return lax.ppermute(value, axis, [(place, place ^ mask) for place in range(count)])


def scatter_sum(part, axis, crossing=jnp.bfloat16):
    count, here = lax.axis_size(axis), lax.axis_index(axis)
    rows = part.shape[0] // count
    total = lax.dynamic_slice_in_dim(part, here * rows, rows)
    for mask in range(1, count):
        block = lax.dynamic_slice_in_dim(part, (here ^ mask) * rows, rows)
        total = total + from_peer(block.astype(crossing), axis, mask).astype(jnp.float32)
    return total


def quad_sum(value, axis):
    value = value.astype(jnp.bfloat16)
    near, middle, far = (from_peer(value, axis, mask).astype(jnp.float32) for mask in (1, 2, 3))
    return (value.astype(jnp.float32) + near) + (middle + far)


def to_all(value, axes):
    count = lax.axis_size(axes)
    value = jnp.broadcast_to(value[None], (count,) + value.shape)
    return lax.all_to_all(value, axes, split_axis=0, concat_axis=0, tiled=True)


PLANE = ("core", "slab", "y")


def sum_blocks(part):
    mine = scatter_sum(scatter_sum(scatter_sum(part, "core", jnp.float32), "slab"), "y", jnp.float32)
    return quad_sum(mine, "z_hi")


def finish_sum(mine, scale):
    mine = (jnp.sum(to_all(mine.astype(jnp.bfloat16), "z_lo").astype(jnp.float32), axis=0) * scale).astype(jnp.bfloat16)
    return to_all(mine, PLANE).reshape(-1, mine.shape[-1]).astype(jnp.float32)


VMEM = pl.BlockSpec(memory_space=pltpu.VMEM)
HBM = pl.BlockSpec(memory_space=pltpu.HBM)
PARTS = 4


def layer_kernel(
    incoming, mixing, mixing_rows, local_sum, inv_degree, weight, cotangent,
    output, aggregated, grad_pre, grad_sum, slot_grad,
    output_rows, aggregated_rows, grad_rows, summed_rows, slots, done,
):
    copies = []

    def leave(source, target):
        copy = pltpu.make_async_copy(source, target, done.at[len(copies)])
        copy.start()
        copies.append(copy)

    inverse = inv_degree[...]
    remote = jnp.dot(mixing[...], incoming[...], preferred_element_type=jnp.float32)
    gathered = ((local_sum[...] + remote) * inverse).astype(jnp.bfloat16)
    aggregated_rows[...] = gathered
    leave(aggregated_rows, aggregated)
    pre_act = jnp.dot(gathered, weight[...], preferred_element_type=jnp.float32)
    gating_value = jax.nn.sigmoid(pre_act)
    scaled = cotangent[...].astype(jnp.float32) * gating_value
    grad = (scaled * (1.0 + pre_act * (1.0 - gating_value))).astype(jnp.bfloat16)
    grad_rows[...] = grad
    leave(grad_rows, grad_pre)
    summed = lax.dot_general(
        grad, weight[...], (((1,), (1,)), ((), ())), preferred_element_type=jnp.float32
    )
    summed = (summed * inverse).astype(jnp.bfloat16)
    summed_rows[...] = summed
    leave(summed_rows, grad_sum)
    rows = slots.shape[0] // PARTS
    for part in range(PARTS):
        span = pl.ds(part * rows, rows)
        slots[span, :] = jnp.dot(
            mixing_rows[span, :], summed, preferred_element_type=jnp.float32
        ).astype(jnp.bfloat16)
        leave(slots.at[span, :], slot_grad.at[span, :])
    output_rows[...] = (pre_act * gating_value).astype(jnp.bfloat16)
    leave(output_rows, output)
    for copy in copies:
        copy.wait()


def layer(incoming, mixing, local_sum, inv_degree, weight, cotangent):
    nodes, slot_count = mixing.shape
    width = weight.shape[0]
    rows = pltpu.HBM((nodes, width), jnp.bfloat16)
    return pl.pallas_call(
        layer_kernel,
        out_shape=(rows, rows, rows, rows, pltpu.HBM((slot_count, width), jnp.bfloat16)),
        in_specs=[VMEM] * 7,
        out_specs=(HBM,) * 5,
        scratch_shapes=[pltpu.VMEM((nodes, width), jnp.bfloat16)] * 4
        + [
            pltpu.VMEM((slot_count, width), jnp.bfloat16),
            pltpu.SemaphoreType.DMA((4 + PARTS,)),
        ],
        compiler_params=pltpu.CompilerParams(vmem_limit_bytes=24 << 20),
        cost_estimate=pl.CostEstimate(
            flops=2 * nodes * width * (2 * slot_count + 2 * width),
            bytes_accessed=6 << 20,
            transcendentals=nodes * width,
        ),
        name="layer",
    )(incoming, mixing, mixing.T, local_sum, inv_degree[:, None], weight, cotangent)


def take_kernel(
    send_rows, send_count, node_feats, outgoing, row_table, counts, feats, taken, ready, done
):
    arrivals = []
    for at, (source, target) in enumerate(
        ((send_rows, row_table), (send_count, counts), (node_feats, feats))
    ):
        copy = pltpu.make_async_copy(source, target, ready.at[at])
        copy.start()
        arrivals.append(copy)
    slot_cap, peer_count = row_table.shape
    nodes, slot_count = feats.shape[0], taken.shape[0]
    slot = lax.broadcasted_iota(jnp.int32, (slot_count, peer_count), 0)
    first = slot_cap * lax.broadcasted_iota(jnp.int32, (slot_count, peer_count), 1)
    place = jnp.where((slot >= first) & (slot < first + slot_cap), 1.0, 0.0)
    slot = lax.broadcasted_iota(jnp.int32, (slot_count, slot_cap), 0)
    column = lax.rem(slot, slot_cap) == lax.broadcasted_iota(jnp.int32, slot.shape, 1)
    arrivals[0].wait()
    arrivals[1].wait()
    rank = lax.broadcasted_iota(jnp.int32, (slot_cap, peer_count), 0)
    live = jnp.where(rank < counts[...], row_table[...], nodes).astype(jnp.float32)
    spread = lax.dot_general(
        place.astype(jnp.bfloat16),
        live.astype(jnp.bfloat16),
        (((1,), (1,)), ((), ())),
        preferred_element_type=jnp.float32,
    )
    spread = jnp.where(column, spread, 0.0).astype(jnp.bfloat16)
    row = jnp.dot(
        spread, jnp.ones((slot_cap, nodes), jnp.bfloat16), preferred_element_type=jnp.float32
    )
    node = lax.broadcasted_iota(jnp.int32, row.shape, 1).astype(jnp.float32)
    chosen = jnp.where(row == node, 1.0, 0.0).astype(jnp.bfloat16)
    arrivals[2].wait()
    rows = slot_count // PARTS
    copies = []
    for part in range(PARTS):
        span = pl.ds(part * rows, rows)
        taken[span, :] = jnp.dot(
            chosen[part * rows : (part + 1) * rows], feats[...], preferred_element_type=jnp.float32
        ).astype(jnp.bfloat16)
        copy = pltpu.make_async_copy(taken.at[span, :], outgoing.at[span, :], done.at[part])
        copy.start()
        copies.append(copy)
    for copy in copies:
        copy.wait()


def take_rows(send_rows, send_count, node_feats):
    peer_count, slot_cap = send_rows.shape
    nodes, width = node_feats.shape
    slots = jax.ShapeDtypeStruct((peer_count * slot_cap, width), jnp.bfloat16)
    return pl.pallas_call(
        take_kernel,
        out_shape=slots,
        in_specs=[HBM] * 3,
        out_specs=HBM,
        scratch_shapes=[
            pltpu.VMEM((slot_cap, peer_count), jnp.int32),
            pltpu.VMEM((1, peer_count), jnp.int32),
            pltpu.VMEM((nodes, width), jnp.bfloat16),
            pltpu.VMEM(slots.shape, slots.dtype),
            pltpu.SemaphoreType.DMA((3,)),
            pltpu.SemaphoreType.DMA((PARTS,)),
        ],
        compiler_params=pltpu.CompilerParams(vmem_limit_bytes=63_400_000),
        cost_estimate=pl.CostEstimate(
            flops=2 * nodes * width * peer_count * slot_cap,
            bytes_accessed=2 << 20,
            transcendentals=0,
        ),
        name="take_rows",
    )(send_rows.T, send_count[None, :], node_feats)


def shards(
    node_feats,
    weight,
    cotangent,
    degrees,
    local_weights,
    local_tiles,
    send_rows,
    send_count,
    recv_target,
    recv_weight,
):
    row_count, feat_width = node_feats.shape
    tile_size = local_weights.shape[2]
    tile_count = row_count // tile_size
    listed = local_tiles.shape[1]
    peer_count = lax.axis_size(DOM)
    slot_cap = send_rows.shape[1]
    slot_count = peer_count * slot_cap
    nodes_all = row_count * lax.axis_size(DOM + ("slab",))
    column_ids = jnp.arange(tile_count, dtype=jnp.int32)
    selector = (local_tiles[:, :, None] == column_ids[None, None, :]).astype(jnp.bfloat16)
    blocks = local_weights.reshape(tile_count, tile_size, listed, tile_size).astype(jnp.bfloat16)
    adjacency = jnp.einsum("ikj,iakb->iajb", selector, blocks, preferred_element_type=jnp.float32)
    adjacency = adjacency.reshape(row_count, row_count).astype(jnp.bfloat16)
    live_slot = jnp.arange(slot_cap, dtype=jnp.int32)[None, :] < send_count[:, None]
    row_ids = jnp.arange(row_count, dtype=jnp.int32)
    slot_ids = jnp.arange(slot_count, dtype=jnp.int32)
    live_rows = jnp.where(live_slot, send_rows, row_count).astype(jnp.bfloat16)
    to_slot = jnp.arange(peer_count, dtype=jnp.int32)[:, None] == slot_ids[None, :] // slot_cap
    spread = lax.dot_general(
        live_rows,
        to_slot.astype(jnp.bfloat16),
        (((0,), (0,)), ((), ())),
        preferred_element_type=jnp.float32,
    )
    own_column = jnp.arange(slot_cap, dtype=jnp.int32)[:, None] == slot_ids[None, :] % slot_cap
    flat_rows = jnp.sum(jnp.where(own_column, spread, 0.0), axis=0)
    owner = (row_ids[:, None] == flat_rows.astype(jnp.int32)[None, :]).astype(jnp.bfloat16)
    outgoing = take_rows(send_rows, send_count, node_feats)
    outgoing = outgoing.reshape(peer_count, slot_cap, feat_width)
    incoming = lax.all_to_all(outgoing, DOM, split_axis=0, concat_axis=0, tiled=True).reshape(
        slot_count, feat_width
    )
    local_sum = jnp.dot(
        adjacency, node_feats, preferred_element_type=jnp.float32
    ) + node_feats.astype(jnp.float32)
    mixing = jnp.sum(
        jnp.where(row_ids[:, None, None] == recv_target[None, :, :], recv_weight[None, :, :], 0),
        axis=2,
    )
    mixing = mixing.astype(jnp.bfloat16)
    inv_degree = 1.0 / degrees.astype(jnp.float32)
    output, aggregated, grad_pre, grad_sum, slot_grad = layer(
        incoming, mixing, local_sum, inv_degree, weight, cotangent
    )
    slot_grad = slot_grad.reshape(peer_count, slot_cap, feat_width)
    slot_grad, aggregated = lax.optimization_barrier((slot_grad, aggregated))
    returned = lax.all_to_all(slot_grad, DOM, split_axis=0, concat_axis=0, tiled=True)
    returned = returned.reshape(slot_count, feat_width)
    weight_part = lax.dot_general(
        aggregated, grad_pre, (((0,), (0,)), ((), ())), preferred_element_type=jnp.float32
    )
    mine = sum_blocks(weight_part)
    returned, mine = lax.optimization_barrier((returned, mine))
    grad_weight = finish_sum(mine, 1.0 / math.sqrt(nodes_all))
    local_back = lax.dot_general(
        adjacency, grad_sum, (((0,), (0,)), ((), ())), preferred_element_type=jnp.float32
    )
    local_back = local_back + grad_sum.astype(jnp.float32)
    remote_back = jnp.dot(owner, returned, preferred_element_type=jnp.float32)
    grad_feats = (local_back + remote_back).astype(jnp.bfloat16)
    return (output, grad_feats, grad_weight)


def solution(mesh):
    slab_count = mesh.shape["slab"]
    split = Mesh(
        mesh.devices.reshape(4, 4, -1, 2, slab_count), ("y", "z_hi", "z_lo", "core", "slab")
    )
    nodes = P(DOM + ("slab",))
    in_specs = (nodes, P(), nodes, nodes, nodes, nodes, nodes, nodes, nodes, nodes)
    out_specs = (nodes, nodes, P())
    return jax.shard_map(shards, mesh=split, in_specs=in_specs, out_specs=out_specs, check_vma=False)
```
